32 devices in a mesh: rep: 2 (over x), node: 2 (over core), local: 8 (over z, y).
Axes of the slice: x: 2, y: 2, z: 4, core: 2. Of those that a mesh axis runs over, the one named last changes fastest.
Arguments:
- tokens: bfloat16 [4608, 7168], P(('rep', 'node', 'local')), parts along dimension 0, may hold values from -6 to 6
- expert_ids: int32 [4608, 8], P(('rep', 'node', 'local')), parts along dimension 0, may hold values from 0 to 255, as said below
- route_scores: float32 [4608, 8], P(('rep', 'node', 'local')), parts along dimension 0, may hold values from 0.05 to 1
- gate_weight: bfloat16 [16, 7168, 512], P(('node', 'local')), may hold values from -0.0625 to 0.0625
- up_weight: bfloat16 [16, 7168, 512], P(('node', 'local')), may hold values from -0.0625 to 0.0625
- down_weight: bfloat16 [16, 512, 7168], P(('node', 'local')), may hold values from -0.125 to 0.125
Outputs:
- moe_out: bfloat16 [4608, 7168], P(('rep', 'node', 'local')), parts along dimension 0
The draws below stay inside these ranges and needn't reach their ends.
There are 2 independent parts, one for each index of `rep`. The reference program is written for one: setup_inputs(seed, part) draws one part's arguments, and reference() takes and returns one part's arrays. A program takes and returns all parts, laid end to end along the dimension named above; an argument that names none is the same for every part. Nothing has to cross between parts.
Inputs may be any that keep to these rules, and one draw needn't show every extreme that they name: `expert_ids`: each row names 8 different experts, two in each of 4 different groups of 32 consecutive experts. A row names at most one expert of the form r * 32 with r below 4. In each aligned block of 144 rows every such expert is named by 1 to 18 rows, and in every draw one of them is named by exactly 18 rows in every block.
All inputs are finite; a program needn't handle non-finite values.
Results may differ from the reference program's by a relative error of at most 0.009.
Values may be sent and summed in bfloat16 or wider, within the bound.
No kernel may reach another device: no remote copies, remote signals or barrier semaphores. Data moves between devices by JAX's collectives and lax.ppermute only.
A program may use at most 128 MiB of HBM per device.

```python
import math
import jax
import jax.numpy as jnp
from jax import lax

D = 7168
H = 2048
GROUPS = 8
TGROUPS = 4
TOP = 8
TEAM = 4
TOK_DEV = 144
CAP = 18
GSIZE = 32
FLIGHT = 4
TOKENS = 2304


def draw_expert_ids(key, part):
    key = jax.random.fold_in(key, 11)
    key_list = jax.random.split(key, 7)
    blocks = TOKENS // TOK_DEV
    counts = jax.random.randint(key_list[0], (blocks, FLIGHT), 1, CAP + 1)
    hottest = jax.random.randint(key_list[1], (), 0, FLIGHT)
    counts = jnp.where(jnp.arange(FLIGHT)[None, :] == hottest, CAP, counts)
    starts = jnp.cumsum(counts, axis=1) - counts
    order_keys = jax.random.randint(key_list[2], (blocks, TOK_DEV), 0, 1 << 20) * TOK_DEV + jnp.arange(TOK_DEV)[None, :]
    rank_of = jnp.argsort(jnp.argsort(order_keys, axis=1), axis=1)
    inside = (rank_of[:, :, None] >= starts[:, None, :]) & (rank_of[:, :, None] < (starts + counts)[:, None, :])
    chosen = jnp.any(inside, axis=2).reshape(TOKENS)
    flight_pick = jnp.sum(inside.astype(jnp.int32) * jnp.arange(FLIGHT)[None, None, :], axis=2).reshape(TOKENS)
    group_keys = jax.random.randint(key_list[3], (TOKENS, GROUPS), 0, 1 << 16) * GROUPS + jnp.arange(GROUPS)[None, :]
    forced = chosen[:, None] & (jnp.arange(GROUPS)[None, :] == flight_pick[:, None])
    group_keys = jnp.where(forced, -1, group_keys)
    group_order = jnp.argsort(group_keys, axis=1)[:, :TGROUPS]
    first_member = jax.random.randint(key_list[4], (TOKENS, TGROUPS), 1, GSIZE)
    second = 1 + (first_member - 1 + jax.random.randint(key_list[5], (TOKENS, TGROUPS), 1, GSIZE - 1)) % (GSIZE - 1)
    lead_group = jnp.arange(TGROUPS)[None, :] == 0
    first_member = jnp.where(lead_group & chosen[:, None], 0, first_member)
    members = jnp.stack([first_member, second], axis=2)
    picked_ids = (group_order[:, :, None] * GSIZE + members).reshape(TOKENS, TOP)
    roll_by = jax.random.randint(key_list[6], (TOKENS, 1), 0, TOP)
    position = (jnp.arange(TOP)[None, :] + roll_by) % TOP
    return jnp.take_along_axis(picked_ids, position, axis=1).astype(jnp.int32)


def levels(key, shape, cuts, smallest, top_value):
    gain, own = 1.0, jax.random.fold_in(key, 6)
    for dim, blocks in cuts:
        draws = jnp.exp(jax.random.uniform(jax.random.fold_in(own, dim), (blocks,), jnp.float32, smallest / len(cuts), top_value / len(cuts)))
        gain = gain * jnp.repeat(draws, shape[dim] // blocks).reshape([-1 if axis == dim else 1 for axis in range(len(shape))])
    return gain


def normal_values(own_key, extent, width, limit, shards=(), held_as=jnp.bfloat16):
    factor_of = levels(own_key, extent, shards, -0.22, 0.18) if shards else 1.0
    result = jax.random.normal(own_key, extent, jnp.float32) * width * factor_of
    return jnp.minimum(jnp.maximum(result, -limit), limit).astype(held_as)


def setup_inputs(seed: int = 0, part: int = 0) -> dict:
    keys = jax.random.split(jax.random.key(seed), 7)
    own_keys = jax.random.split(jax.random.fold_in(keys[6], part), 7)
    tokens = normal_values(own_keys[0], (TOKENS, D), 1.0, 6.0, ((0, 16),))
    expert_ids = draw_expert_ids(jax.random.fold_in(jax.random.fold_in(keys[6], part), 71), part)
    route_scores = jnp.clip(jnp.exp(math.log(1.0) - 2.9957323 * jax.random.uniform(own_keys[2], (TOKENS, TOP), jnp.float32) ** levels(own_keys[2], (TOKENS, TOP), ((0, 16),), -0.2, 0.2)), 0.05, 1.0)
    gate_weight = normal_values(keys[3], (FLIGHT * TEAM, D, H // TEAM), D ** -0.5, 0.0625, ((0, 16),))
    up_weight = normal_values(keys[4], (FLIGHT * TEAM, D, H // TEAM), D ** -0.5, 0.0625, ((0, 16),))
    down_weight = normal_values(keys[5], (FLIGHT * TEAM, H // TEAM, D), H ** -0.5, 0.125, ((0, 16),))
    return {"tokens": tokens, "expert_ids": expert_ids, "route_scores": route_scores, "gate_weight": gate_weight, "up_weight": up_weight, "down_weight": down_weight}


route_scale = 2.5


def pack_matrix(expert_ids, flight_ids):
    matched = jnp.any(expert_ids[:, None, :] == flight_ids[None, :, None], axis=2)
    slot_index = jnp.cumsum(matched.astype(jnp.int32), axis=0).astype(jnp.int32) - 1
    capacity_iota = jnp.arange(CAP, dtype=jnp.int32)
    picked = matched.T[:, None, :] & (slot_index.T[:, None, :] == capacity_iota[None, :, None])
    return picked


def token_weights(expert_ids, route_scores, flight_ids):
    gate_values = route_scale * route_scores / jnp.sum(route_scores, axis=1, keepdims=True)
    hit_mask = (expert_ids[:, :, None] == flight_ids[None, None, :]).astype(jnp.float32)
    return jnp.sum(gate_values[:, :, None] * hit_mask, axis=1)


def reference(tokens, expert_ids, route_scores, gate_weight, up_weight, down_weight):
    device_count = TOKENS // TOK_DEV
    flight_ids = jnp.arange(FLIGHT, dtype=jnp.int32) * GSIZE
    block_ids = expert_ids.reshape(device_count, TOK_DEV, TOP)
    picked = jax.vmap(lambda one_block: pack_matrix(one_block, flight_ids))(block_ids).astype(jnp.float32)
    block_tokens = tokens.reshape(device_count, TOK_DEV, D).astype(jnp.float32)
    dispatched = jnp.einsum("bfct,btd->fbcd", picked, block_tokens).astype(jnp.bfloat16)
    outputs = []
    for expert in range(FLIGHT):
        row_block = dispatched[expert].reshape(device_count * CAP, D)

        def add_slice(total, slice_index):
            entry = (slice_index + expert * TEAM).astype(jnp.int32)
            gate_here = lax.dynamic_index_in_dim(gate_weight, entry, 0, keepdims=False)
            up_here = lax.dynamic_index_in_dim(up_weight, entry, 0, keepdims=False)
            down_here = lax.dynamic_index_in_dim(down_weight, entry, 0, keepdims=False)
            gate_part = jnp.dot(row_block, gate_here, preferred_element_type=jnp.float32)
            up_part = jnp.dot(row_block, up_here, preferred_element_type=jnp.float32)
            hidden = (jax.nn.silu(gate_part) * up_part).astype(jnp.bfloat16)
            partial_value = jnp.dot(hidden, down_here, preferred_element_type=jnp.float32).astype(jnp.bfloat16)
            return total + partial_value.astype(jnp.float32), None

        summed, _ = lax.scan(add_slice, jnp.zeros((device_count * CAP, D), jnp.float32), jnp.arange(TEAM, dtype=jnp.int32))
        outputs.append(summed.astype(jnp.bfloat16).reshape(device_count, CAP, D))
    expert_out = jnp.stack(outputs, axis=0).astype(jnp.float32)
    weights_now = token_weights(expert_ids, route_scores, flight_ids).reshape(device_count, TOK_DEV, FLIGHT)
    coefficient = picked * jnp.transpose(weights_now, (0, 2, 1))[:, :, None, :]
    combined = jnp.einsum("bfct,fbcd->btd", coefficient, expert_out)
    return combined.reshape(TOKENS, D).astype(jnp.bfloat16)
```

```python
import jax
import jax.numpy as jnp
from jax import lax
from jax.sharding import PartitionSpec as P

TEAM = 4
CAP = 18
GSIZE = 32
ROW_TILE = 8

route_scale = 2.5


def swap(value, axis, pairs):
    return lax.ppermute(value, axis, pairs)


def total(*terms):
    summed = terms[0].astype(jnp.float32)
    for term in terms[1:]:
        summed = summed + term.astype(jnp.float32)
    return summed.astype(jnp.bfloat16)


def local(tokens, expert_ids, route_scores, gate_weight, up_weight, down_weight):
    model_width = tokens.shape[1]
    half = model_width // 2
    node_count = lax.axis_size("node")
    local_count = lax.axis_size("local")
    teams = local_count // TEAM
    node = lax.axis_index("node")
    team = lax.axis_index("local") // TEAM

    slots = -(-(node_count * CAP) // ROW_TILE) * ROW_TILE
    offsets = [(n, d) for n in range(node_count) for d in range(teams)]
    flight_ids = jnp.stack(
        [((node + n) % node_count * teams + (team + d) % teams) * GSIZE for n, d in offsets]
    ).astype(jnp.int32)

    hits = expert_ids[:, None, :] == flight_ids[None, :, None]
    matched = jnp.any(hits, axis=2)
    slot_index = jnp.cumsum(matched.astype(jnp.int32), axis=0) - 1 + CAP * node
    slot_iota = jnp.arange(slots, dtype=jnp.int32)
    picked = matched.T[:, None, :] & (slot_index.T[:, None, :] == slot_iota[None, :, None])
    picked = picked.astype(jnp.bfloat16)
    dispatched = jnp.einsum(
        "fct,td->fcd", picked, tokens, preferred_element_type=jnp.float32
    ).astype(jnp.bfloat16)

    cores = [(n, (n + 1) % node_count) for n in range(node_count)]
    flip_y = [(i, i ^ 1) for i in range(local_count)]
    flip_z = [(i, i ^ 2) for i in range(local_count)]

    def to_team(d):
        return [(i, (i + d * TEAM) % local_count) for i in range(local_count)]

    got = swap(dispatched[teams:], "node", cores)
    blocks = dispatched[:teams] + got

    own = blocks[0]
    own_y = swap(own, "local", flip_y)
    own_z = swap(own, "local", flip_z)
    own_d = jnp.concatenate(
        [
            swap(own_y[:, :half], "local", flip_z),
            swap(own_z[:, half:], "local", flip_y),
        ],
        axis=1,
    )
    rows = [own, own_y, own_z, own_d]
    for d in range(1, teams):
        far = swap(blocks[d], "local", to_team(d))
        far_z = swap(far, "local", flip_z)
        far_y = swap(far, "local", flip_y)
        far_d = swap(far_z, "local", flip_y)
        rows += [far, far_y, far_z, far_d]

    row_block = jnp.concatenate(rows, axis=0)
    gate_part = jnp.dot(row_block, gate_weight[0], preferred_element_type=jnp.float32)
    up_part = jnp.dot(row_block, up_weight[0], preferred_element_type=jnp.float32)
    hidden = (jax.nn.silu(gate_part) * up_part).astype(jnp.bfloat16)
    partial = jnp.dot(hidden, down_weight[0], preferred_element_type=jnp.float32).astype(
        jnp.bfloat16
    )
    parts = [partial[i * slots : (i + 1) * slots] for i in range(TEAM * teams)]

    own, own_y, own_z, own_d = parts[:TEAM]
    back_z = swap(own_d[:, :half], "local", flip_z)
    back_y = swap(own_d[:, half:], "local", flip_y)
    own_y = jnp.concatenate([total(own_y[:, :half], back_z), own_y[:, half:]], axis=1)
    own_z = jnp.concatenate([own_z[:, :half], total(own_z[:, half:], back_y)], axis=1)
    sums = [total(own, swap(own_y, "local", flip_y), swap(own_z, "local", flip_z))]
    for d in range(1, teams):
        far, far_y, far_z, far_d = parts[TEAM * d : TEAM * (d + 1)]
        far_z = total(far_z, swap(far_d, "local", flip_y))
        far = total(far, swap(far_y, "local", flip_y), swap(far_z, "local", flip_z))
        sums.append(swap(far, "local", to_team(teams - d)))
    mine = jnp.stack(sums)
    theirs = swap(mine, "node", cores)
    returned = jnp.concatenate([mine, theirs]).reshape(-1, model_width)

    gate_values = route_scale * route_scores / jnp.sum(route_scores, axis=1, keepdims=True)
    weight = jnp.sum(gate_values * jnp.any(hits, axis=1), axis=1)
    placed = jnp.dot(
        picked.reshape(-1, picked.shape[2]).T, returned, preferred_element_type=jnp.float32
    )
    return (weight[:, None] * placed).astype(jnp.bfloat16)


def solution(mesh):
    in_specs = (
        P(("rep", "node", "local"), None),
        P(("rep", "node", "local"), None),
        P(("rep", "node", "local"), None),
        P(("node", "local"), None, None),
        P(("node", "local"), None, None),
        P(("node", "local"), None, None),
    )
    out_specs = P(("rep", "node", "local"), None)
    return jax.shard_map(local, mesh=mesh, in_specs=in_specs, out_specs=out_specs, check_vma=False)
```

```python
import functools

import jax
import jax.numpy as jnp
from jax import lax
from jax.experimental import pallas as pl
from jax.experimental.pallas import tpu as pltpu
from jax.sharding import PartitionSpec as P

TEAM = 4
CAP = 18
GSIZE = 32
CHUNKS = 2
STACK = 2

route_scale = 2.5
VMEM = pl.BlockSpec(memory_space=pltpu.VMEM)
HBM = pl.BlockSpec(memory_space=pl.ANY)


def dot(a, b):
    return jnp.dot(a, b, preferred_element_type=jnp.float32)


def params(mib):
    return pltpu.CompilerParams(vmem_limit_bytes=mib << 20)


def pack_kernel(pick_ref, tokens_ref, *out_refs):
    experts = len(out_refs)
    rows, width = out_refs[0].shape[1:]
    for c in range(CHUNKS):
        acc = None
        for q in range(STACK):
            first = (c * STACK + q) * width
            term = dot(pick_ref[q], tokens_ref[:, first : first + width])
            acc = term if acc is None else acc + term
        acc = acc.astype(jnp.bfloat16)
        for e in range(experts):
            out_refs[e][c] = acc[e * rows : (e + 1) * rows]


def expert_kernel(spread_ref, place_ref, *refs):
    blocks = refs[: CHUNKS * TEAM]
    gate_hbm, up_hbm, down_hbm = refs[CHUNKS * TEAM : CHUNKS * TEAM + 3]
    outs = refs[CHUNKS * TEAM + 3 : 2 * CHUNKS * TEAM + 3]
    gate, up, down, sems = refs[2 * CHUNKS * TEAM + 3 :]
    width = blocks[0].shape[1]
    pieces = CHUNKS * STACK
    copies = []
    for p in range(pieces):
        span = pl.ds(p * width, width)
        copies.append(
            (
                pltpu.make_async_copy(gate_hbm.at[0, span], gate.at[p], sems.at[0, p]),
                pltpu.make_async_copy(up_hbm.at[0, span], up.at[p], sems.at[1, p]),
            )
        )
    downs = [
        pltpu.make_async_copy(
            down_hbm.at[0, :, pl.ds(p * width, width)], down.at[p], sems.at[2, p]
        )
        for p in range(pieces)
    ]
    for pair in copies:
        for copy in pair:
            copy.start()
    for copy in downs:
        copy.start()
    gate_part = up_part = None
    for c in range(CHUNKS):
        stacked = jnp.concatenate([blocks[c * TEAM + b][...] for b in range(TEAM)], axis=0)
        for q in range(STACK):
            p = c * STACK + q
            rows = dot(spread_ref[q], stacked).astype(jnp.bfloat16)
            copies[p][0].wait()
            copies[p][1].wait()
            gate_term = dot(rows, gate[p])
            up_term = dot(rows, up[p])
            gate_part = gate_term if gate_part is None else gate_part + gate_term
            up_part = up_term if up_part is None else up_part + up_term
    hidden = gate_part / (1.0 + jnp.exp(-gate_part)) * up_part
    hidden = hidden.astype(jnp.bfloat16)
    placed = [dot(place_ref[q], hidden).astype(jnp.bfloat16) for q in range(STACK)]
    count = outs[0].shape[0]
    for c in range(CHUNKS):
        acc = None
        for q in range(STACK):
            p = c * STACK + q
            downs[p].wait()
            term = dot(placed[q], down[p])
            acc = term if acc is None else acc + term
        acc = acc.astype(jnp.bfloat16)
        for b in range(TEAM):
            outs[c * TEAM + b][...] = acc[b * count : (b + 1) * count]


def final_kernel(pick_ref, weight_ref, *refs):
    blocks, out_ref = refs[:-1], refs[-1]
    experts = len(blocks) // CHUNKS
    width = blocks[0].shape[1]
    for c in range(CHUNKS):
        stacked = jnp.concatenate(
            [blocks[c * experts + e][...] for e in range(experts)], axis=0
        )
        for q in range(STACK):
            first = (c * STACK + q) * width
            placed = dot(pick_ref[q], stacked)
            out_ref[:, first : first + width] = (placed * weight_ref[...]).astype(jnp.bfloat16)


def total(*terms):
    summed = terms[0].astype(jnp.float32)
    for term in terms[1:]:
        summed = summed + term.astype(jnp.float32)
    return summed.astype(jnp.bfloat16)


def local(tokens, expert_ids, route_scores, gate_weight, up_weight, down_weight):
    token_count, model_width = tokens.shape
    node_count = lax.axis_size("node")
    local_count = lax.axis_size("local")
    teams = local_count // TEAM
    flight = node_count * teams
    node = lax.axis_index("node")
    team = lax.axis_index("local") // TEAM
    slots = node_count * CAP
    rows = STACK * slots
    width = model_width // (CHUNKS * STACK)
    block = jax.ShapeDtypeStruct((rows, width), jnp.bfloat16)

    offsets = [(n, d) for n in range(node_count) for d in range(teams)]
    flight_ids = jnp.stack(
        [((node + n) % node_count * teams + (team + d) % teams) * GSIZE for n, d in offsets]
    ).astype(jnp.int32)
    hits = expert_ids[:, None, :] == flight_ids[None, :, None]
    matched = jnp.any(hits, axis=2)
    slot_index = jnp.cumsum(matched.astype(jnp.int32), axis=0) - 1 + CAP * node
    place = jnp.arange(rows, dtype=jnp.int32)
    stack_of, slot_of = place // slots, place % slots
    chosen = matched.T[:, None, :] & (slot_index.T[:, None, :] == slot_of[None, :, None])
    pick = chosen[None] & (stack_of[None, None, :, None] == jnp.arange(STACK)[:, None, None, None])
    pick = pick.astype(jnp.bfloat16).reshape(STACK, flight * rows, token_count)
    pick_back = jnp.swapaxes(pick, 1, 2)
    gate_values = route_scale * route_scores / jnp.sum(route_scores, axis=1, keepdims=True)
    weight = jnp.sum(gate_values * jnp.any(hits, axis=1), axis=1)[:, None]

    index = jnp.arange(TEAM * rows, dtype=jnp.int32)
    target = index // rows * slots + index % slots
    stack_at = index % rows // slots
    line = jnp.arange(TEAM * slots, dtype=jnp.int32)
    spread = jnp.stack(
        [(line[:, None] == target[None]) & (stack_at[None] == q) for q in range(STACK)]
    ).astype(jnp.bfloat16)
    spread_back = jnp.swapaxes(spread, 1, 2)

    cores = [(n, (n + 1) % node_count) for n in range(node_count)]
    flip_y = [(i, i ^ 1) for i in range(local_count)]
    flip_z = [(i, i ^ 2) for i in range(local_count)]

    def swap_core(value):
        return lax.ppermute(value, "node", cores)

    def swap_y(value):
        return lax.ppermute(value, "local", flip_y)

    def swap_z(value):
        return lax.ppermute(value, "local", flip_z)

    def to_team(value, d):
        pairs = [(i, (i + d * TEAM) % local_count) for i in range(local_count)]
        return lax.ppermute(value, "local", pairs)

    pair = jax.ShapeDtypeStruct((CHUNKS, rows, width), jnp.bfloat16)
    packed = pl.pallas_call(
        pack_kernel,
        out_shape=[pair] * flight,
        in_specs=[VMEM] * 2,
        out_specs=[VMEM] * flight,
        compiler_params=params(40),
        name="pack",
    )(pick, tokens)

    def experts(blocks):
        scratch = (CHUNKS * STACK, width, gate_weight.shape[2])
        return pl.pallas_call(
            expert_kernel,
            out_shape=[block] * (CHUNKS * TEAM),
            in_specs=[VMEM] * (2 + CHUNKS * TEAM) + [HBM] * 3,
            out_specs=[VMEM] * (CHUNKS * TEAM),
            scratch_shapes=[
                pltpu.VMEM(scratch, jnp.bfloat16),
                pltpu.VMEM(scratch, jnp.bfloat16),
                pltpu.VMEM((scratch[0], scratch[2], scratch[1]), jnp.bfloat16),
                pltpu.SemaphoreType.DMA((3, CHUNKS * STACK)),
            ],
            compiler_params=params(48),
            cost_estimate=pl.CostEstimate(
                flops=6 * TEAM * slots * model_width * gate_weight.shape[2],
                bytes_accessed=6 * model_width * gate_weight.shape[2],
                transcendentals=0,
            ),
            name="experts",
        )(spread, spread_back, *blocks, gate_weight, up_weight, down_weight)

    far = {}
    for d in range(1, teams):
        got = swap_core(packed[teams + d])
        mine = packed[d] + got
        far[d] = [to_team(mine[c], d) for c in range(CHUNKS)]
    got = swap_core(packed[teams])
    mine = packed[0] + got
    own = [mine[c] for c in range(CHUNKS)]
    own_y = [swap_y(v) for v in own]
    own_z = [swap_z(v) for v in own]
    own_d = [swap_z(own_y[0]), swap_y(own_z[1])]
    own_parts = experts([v[c] for c in range(CHUNKS) for v in (own, own_y, own_z, own_d)])

    far_parts = {}
    for d in range(1, teams):
        blocks = []
        for c in range(CHUNKS):
            x = far[d][c]
            x_z = swap_z(x)
            x_y = swap_y(x)
            x_d = swap_y(x_z)
            blocks += [x, x_y, x_z, x_d]
        far_parts[d] = experts(blocks)

    sums = {}
    for d in range(1, teams):
        for c in range(CHUNKS):
            x, x_y, x_z, x_d = far_parts[d][c * TEAM : (c + 1) * TEAM]
            x_z = total(x_z, swap_y(x_d))
            x = total(x, swap_y(x_y), swap_z(x_z))
            sums[d, c] = to_team(x, teams - d)
    (a, a_y, a_z, a_d), (b, b_y, b_z, b_d) = own_parts[:TEAM], own_parts[TEAM:]
    a_y = total(a_y, swap_z(a_d))
    b_z = total(b_z, swap_y(b_d))
    sums[0, 0] = total(a, swap_y(a_y), swap_z(a_z))
    sums[0, 1] = total(b, swap_y(b_y), swap_z(b_z))
    theirs = {key: swap_core(v) for key, v in sums.items()}
    returned = [
        part[d, c] for c in range(CHUNKS) for part in (sums, theirs) for d in range(teams)
    ]
    return pl.pallas_call(
        final_kernel,
        out_shape=jax.ShapeDtypeStruct(tokens.shape, jnp.bfloat16),
        in_specs=[VMEM] * (2 + len(returned)),
        out_specs=VMEM,
        compiler_params=params(40),
        name="combine",
    )(pick_back, weight, *returned)


def solution(mesh):
    in_specs = (
        P(("rep", "node", "local"), None),
        P(("rep", "node", "local"), None),
        P(("rep", "node", "local"), None),
        P(("node", "local"), None, None),
        P(("node", "local"), None, None),
        P(("node", "local"), None, None),
    )
    out_specs = P(("rep", "node", "local"), None)
    return jax.shard_map(local, mesh=mesh, in_specs=in_specs, out_specs=out_specs, check_vma=False)
```

```python
import jax
import jax.numpy as jnp
from jax import lax
from jax.experimental import pallas as pl
from jax.experimental.pallas import tpu as pltpu
from jax.sharding import PartitionSpec as P

TEAM = 4
CAP = 18
GSIZE = 32
STACK = 4
COST = 60

route_scale = 2.5
VMEM = pl.BlockSpec(memory_space=pltpu.VMEM)
SMEM = pl.BlockSpec(memory_space=pltpu.SMEM)
HBM = pl.BlockSpec(memory_space=pltpu.HBM)


def dot(a, b):
    return jnp.dot(a, b, preferred_element_type=jnp.float32)


def params(mib):
    return pltpu.CompilerParams(vmem_limit_bytes=mib << 20)


def pieces_of(value, q):
    return value[q * CAP : (q + 1) * CAP]


def pack_kernel(flight_ref, ids_ref, scores_ref, tokens_hbm, *refs):
    tokens, sems = refs[-2:]
    outs, pick_ref, weight_ref = refs[:-4], refs[-4], refs[-3]
    experts = len(outs)
    width = outs[0].shape[1]
    copies = [
        pltpu.make_async_copy(
            tokens_hbm.at[:, pl.ds(q * width, width)], tokens.at[q], sems.at[q]
        )
        for q in range(STACK)
    ]
    for copy in copies:
        copy.start()
    ids = ids_ref[...]
    scores = scores_ref[...]
    count = ids.shape[1]
    earlier = lax.broadcasted_iota(jnp.int32, (count, count), 0) < lax.broadcasted_iota(
        jnp.int32, (count, count), 1
    )
    earlier = jnp.where(earlier, 1.0, 0.0).astype(jnp.bfloat16)
    slot = lax.broadcasted_iota(jnp.int32, (CAP, count), 0).astype(jnp.float32)
    hits = [jnp.where(ids == flight_ref[e], 1.0, 0.0) for e in range(experts)]
    rows = jnp.concatenate([jnp.sum(hit, axis=0, keepdims=True) for hit in hits], axis=0)
    ranks = dot(rows.astype(jnp.bfloat16), earlier)
    pick = jnp.concatenate(
        [
            jnp.where(slot == ranks[e : e + 1], rows[e : e + 1], 0.0)
            for e in range(experts)
        ],
        axis=0,
    )
    pick_ref[...] = pick.astype(jnp.bfloat16)
    gate_values = route_scale * scores / jnp.sum(scores, axis=0, keepdims=True)
    weight = jnp.sum(gate_values * sum(hits), axis=0, keepdims=True)
    weight_ref[...] = jnp.sum(pick * weight, axis=1, keepdims=True)
    pick = pick.astype(jnp.bfloat16)
    parts = []
    for q in range(STACK):
        copies[q].wait()
        parts.append(dot(pick, tokens[q]).astype(jnp.bfloat16))
    for e in range(experts):
        outs[e][...] = jnp.concatenate([p[e * CAP : (e + 1) * CAP] for p in parts], axis=0)


def load_kernel(gate_hbm, up_hbm, down_hbm, gate, up, down, sems):
    width = gate.shape[1]
    copies = []
    for q in range(STACK):
        span = pl.ds(q * width, width)
        copies += [
            pltpu.make_async_copy(gate_hbm.at[0, span], gate.at[q], sems.at[0, q]),
            pltpu.make_async_copy(up_hbm.at[0, span], up.at[q], sems.at[1, q]),
            pltpu.make_async_copy(down_hbm.at[0, :, span], down.at[q], sems.at[2, q]),
        ]
    for copy in copies:
        copy.start()
    for copy in copies:
        copy.wait()


def expert_kernel(gate, up, down, *refs):
    count = len(refs) // 2
    blocks, outs = refs[:count], refs[count:]
    values = [block[...] for block in blocks]
    gate_part = up_part = None
    for q in range(STACK):
        rows = jnp.concatenate([pieces_of(value, q) for value in values], axis=0)
        gate_term = dot(rows, gate[q])
        up_term = dot(rows, up[q])
        gate_part = gate_term if gate_part is None else gate_part + gate_term
        up_part = up_term if up_part is None else up_part + up_term
    hidden = gate_part / (1.0 + jnp.exp(-gate_part)) * up_part
    hidden = hidden.astype(jnp.bfloat16)
    parts = [dot(hidden, down[q]).astype(jnp.bfloat16) for q in range(STACK)]
    for b in range(count):
        outs[b][...] = jnp.concatenate([p[b * CAP : (b + 1) * CAP] for p in parts], axis=0)


def final_kernel(pick_ref, weight_ref, *refs):
    blocks, out_ref = refs[:-1], refs[-1]
    width = blocks[0].shape[1]
    values = [block[...] for block in blocks]
    pick = pick_ref[...]
    for q in range(STACK):
        rows = jnp.concatenate([pieces_of(value, q) for value in values], axis=0)
        rows = (rows.astype(jnp.float32) * weight_ref[...]).astype(jnp.bfloat16)
        placed = lax.dot_general(
            pick, rows, (((0,), (0,)), ((), ())), preferred_element_type=jnp.float32
        )
        out_ref[:, q * width : (q + 1) * width] = placed.astype(jnp.bfloat16)


def in_hbm(value):
    return pltpu.with_memory_space_constraint(value, pltpu.HBM)


def after(value, *done):
    return lax.optimization_barrier((value, *done))[0]


class Line:
    def __init__(self, send):
        self.send, self.done = send, []

    def __call__(self, name, value, *done):
        self.done.append(self.send(name, value, *done, *self.done[-2:-1]))
        return self.done[-1]


def total(*terms):
    summed = terms[0].astype(jnp.float32)
    for term in terms[1:]:
        summed = summed + term.astype(jnp.float32)
    return summed.astype(jnp.bfloat16)


def local(tokens, expert_ids, route_scores, gate_weight, up_weight, down_weight):
    token_count, model_width = tokens.shape
    hidden_width = gate_weight.shape[2]
    nodes = lax.axis_size("node")
    places = lax.axis_size("local")
    teams = places // TEAM
    flight = nodes * teams
    node = lax.axis_index("node")
    team = lax.axis_index("local") // TEAM
    width = model_width // STACK
    block = jax.ShapeDtypeStruct((STACK * CAP, width), jnp.bfloat16)

    offsets = [(n, d) for n in range(nodes) for d in range(teams)]
    flight_ids = jnp.stack(
        [((node + n) % nodes * teams + (team + d) % teams) * GSIZE for n, d in offsets]
    ).astype(jnp.int32)
    packed = pl.pallas_call(
        pack_kernel,
        out_shape=[block] * flight
        + [
            jax.ShapeDtypeStruct((flight * CAP, token_count), jnp.bfloat16),
            jax.ShapeDtypeStruct((flight * CAP, 1), jnp.float32),
        ],
        in_specs=[SMEM] + [VMEM] * 2 + [HBM],
        out_specs=[VMEM] * (flight + 2),
        scratch_shapes=[
            pltpu.VMEM((STACK, token_count, width), jnp.bfloat16),
            pltpu.SemaphoreType.DMA((STACK,)),
        ],
        compiler_params=params(20),
        name="pack",
    )(flight_ids, expert_ids.T, route_scores.T, in_hbm(tokens))
    pick, weight = packed[flight:]
    packed = dict(zip(offsets, packed))

    def experts(blocks, *done):
        blocks = [after(blocks[0], *done), *blocks[1:]]
        return pl.pallas_call(
            expert_kernel,
            out_shape=[block] * len(blocks),
            in_specs=[VMEM] * (3 + len(blocks)),
            out_specs=[VMEM] * len(blocks),
            compiler_params=params(20),
            cost_estimate=pl.CostEstimate(
                flops=COST * len(blocks) * CAP * model_width * hidden_width,
                bytes_accessed=COST * model_width * hidden_width,
                transcendentals=0,
            ),
            name="experts",
        )(*weights, *blocks)

    def send(value, n, d, flip, *done):
        pairs = [
            (
                i * places + j,
                (i + n) % nodes * places + ((j + d * TEAM) % places ^ flip),
            )
            for i in range(nodes)
            for j in range(places)
        ]
        return lax.ppermute(after(value, *done) if done else value, ("node", "local"), pairs)

    def swap_y(name, value, *done):
        with jax.named_scope(name):
            return send(value, 0, 0, 1, *done)

    def swap_z(name, value, *done):
        with jax.named_scope(name):
            return send(value, 0, 0, 2, *done)

    def shift(name, value, n, d, *done):
        with jax.named_scope(name):
            return send(value, n, d, 0, *done)

    fars = [(n, d) for d in range(1, teams) for n in range(nodes)]
    own = [shift("own_core", packed[n, 0], n, 0) if n else packed[0, 0] for n in range(nodes)]
    weights = pl.pallas_call(
        load_kernel,
        out_shape=[
            pltpu.VMEM((STACK, width, hidden_width), jnp.bfloat16),
            pltpu.VMEM((STACK, width, hidden_width), jnp.bfloat16),
            pltpu.VMEM((STACK, hidden_width, width), jnp.bfloat16),
        ],
        in_specs=[HBM] * 3,
        out_specs=[VMEM] * 3,
        scratch_shapes=[pltpu.SemaphoreType.DMA((3, STACK))],
        compiler_params=params(20),
        cost_estimate=pl.CostEstimate(
            flops=0, bytes_accessed=COST * model_width * hidden_width, transcendentals=0
        ),
        name="load",
    )(in_hbm(after(gate_weight, own[-1])), in_hbm(up_weight), in_hbm(down_weight))

    y, z = Line(swap_y), Line(swap_z)
    own_y = [y("own_y%d" % n, own[n], own[-1]) for n in reversed(range(nodes))][::-1]
    own_z, own_d = [None] * nodes, [None] * nodes
    own_z[-1] = z("own_z%d" % (nodes - 1), own[-1])
    spread = {}
    x = None
    for i, key in enumerate(fars):
        tag = "far%d_" % i
        x = shift(tag, packed[key], *key, *([x, weights[0]] if i else []))
        x_z = z(tag + "z", x, weights[0], own_z[-1])
        if i:
            x_y = y(tag + "y", x)
        else:
            x_y = y(tag + "y", x, weights[0])
            for n in range(1, nodes, 2):
                own_d[n] = y("own_d%d" % n, own_z[n])
        x_d = y(tag + "d", x_z)
        spread[key] = (x, x_y, x_z, x_d)
    for n in range(nodes - 1):
        own_z[n] = z("own_z%d" % n, own[n])
    for n in range(0, nodes, 2):
        own_d[n] = z("own_d%d" % n, own_y[n])

    parts, back = {}, {}
    own_blocks = [v for n in range(nodes) for v in (own[n], own_y[n], own_z[n], own_d[n])]
    last = None
    for i, key in enumerate(fars):
        parts[key] = experts(spread[key], *([last] if i else []))
        last = parts[key][0]
    own_parts = experts(own_blocks, last)
    own_parts = [own_parts[n * TEAM : (n + 1) * TEAM] for n in range(nodes)]
    z = Line(swap_z)
    mine_y, mine_z, mine_d = [None] * nodes, [None] * nodes, [None] * nodes
    for n in range(0, nodes, 2):
        mine_d[n] = z("mine%d_d" % n, own_parts[n][3])
    for i, key in enumerate(fars):
        tag = "back%d_" % i
        x, x_y, x_z, x_d = parts[key]
        x_d = y(tag + "d", x_d)
        x_y = y(tag + "y", x_y)
        x_z = z(tag + "z", total(x_z, x_d))
        n, d = key
        back[key] = shift(tag, total(x, x_y, x_z), nodes - n, teams - d)
        if i == 0:
            mine_z[0] = z("mine0_z", own_parts[0][2])
    for n in range(1, nodes, 2):
        mine_d[n] = y("mine%d_d" % n, own_parts[n][3])
    for n in range(nodes):
        x, a_y, a_z, a_d = own_parts[n]
        tag = "mine%d_" % n
        if n % 2:
            a_z = total(a_z, mine_d[n])
        else:
            a_y = total(a_y, mine_d[n])
        a_y = y(tag + "y", a_y)
        a_z = z(tag + "z", a_z) if mine_z[n] is None else mine_z[n]
        x = total(x, a_y, a_z)
        back[n, 0] = shift("mine_core", x, nodes - n, 0) if n else x

    return pl.pallas_call(
        final_kernel,
        out_shape=jax.ShapeDtypeStruct(tokens.shape, jnp.bfloat16),
        in_specs=[VMEM] * (2 + flight),
        out_specs=VMEM,
        compiler_params=params(20),
        name="combine",
    )(pick, weight, *[back[key] for key in offsets])


def solution(mesh):
    in_specs = (
        P(("rep", "node", "local"), None),
        P(("rep", "node", "local"), None),
        P(("rep", "node", "local"), None),
        P(("node", "local"), None, None),
        P(("node", "local"), None, None),
        P(("node", "local"), None, None),
    )
    out_specs = P(("rep", "node", "local"), None)
    return jax.shard_map(local, mesh=mesh, in_specs=in_specs, out_specs=out_specs, check_vma=False)
```

```python
import jax
import jax.numpy as jnp
from jax import lax
from jax.experimental import pallas as pl
from jax.experimental.pallas import tpu as pltpu
from jax.sharding import PartitionSpec as P

TEAM = 4
CAP = 18
GSIZE = 32
STACK = 4
COST = 60

AFTER = {
    "load": ("own1",),
    "own_y0": ("own1",),
    "own_z0": ("own_z1",),
    "own_d0": ("own_z0",),
    "own_d1": ("own_y0",),
    "far0_d": ("far0_y",),
    "far0_y": ("load", "own_y1"),
    "far0_z": ("load", "own_z1"),
    "far1": ("far0", "load"),
    "far1_d": ("far0_d",),
    "far1_experts": ("own_experts",),
    "far1_y": ("own_d1",),
    "far1_z": ("load", "own_z1"),
    "own_experts": ("far0_experts",),
    "back0_y": ("back0_d",),
    "back1_y": ("back0_y",),
    "back1_z": ("back0_z",),
    "mine_d1": ("far1_d",),
    "mine_y0": ("back1_y",),
    "mine_y1": ("back1_y",),
    "mine_z0": ("back0_z",),
    "mine_z1": ("back0_z",),
}

route_scale = 2.5
VMEM = pl.BlockSpec(memory_space=pltpu.VMEM)
SMEM = pl.BlockSpec(memory_space=pltpu.SMEM)
HBM = pl.BlockSpec(memory_space=pltpu.HBM)


def dot(a, b):
    return jnp.dot(a, b, preferred_element_type=jnp.float32)


def params(mib):
    return pltpu.CompilerParams(vmem_limit_bytes=mib << 20)


def pieces_of(value, q):
    return value[q * CAP : (q + 1) * CAP]


def pack_kernel(flight_ref, ids_hbm, scores_hbm, tokens_hbm, *refs):
    tokens, ids_ref, scores_ref, sems = refs[-4:]
    outs, pick_ref, weight_ref = refs[:-6], refs[-6], refs[-5]
    experts = len(outs)
    width = outs[0].shape[1]
    copies = [
        pltpu.make_async_copy(
            tokens_hbm.at[:, pl.ds(q * width, width)], tokens.at[q], sems.at[q]
        )
        for q in range(STACK)
    ]
    small = [
        pltpu.make_async_copy(ids_hbm, ids_ref, sems.at[STACK]),
        pltpu.make_async_copy(scores_hbm, scores_ref, sems.at[STACK + 1]),
    ]
    for copy in small + copies:
        copy.start()
    for copy in small:
        copy.wait()
    ids = ids_ref[...]
    scores = scores_ref[...]
    count = ids.shape[1]
    earlier = lax.broadcasted_iota(jnp.int32, (count, count), 0) < lax.broadcasted_iota(
        jnp.int32, (count, count), 1
    )
    earlier = jnp.where(earlier, 1.0, 0.0).astype(jnp.bfloat16)
    slot = lax.broadcasted_iota(jnp.int32, (CAP, count), 0).astype(jnp.float32)
    hits = [jnp.where(ids == flight_ref[e], 1.0, 0.0) for e in range(experts)]
    rows = jnp.concatenate([jnp.sum(hit, axis=0, keepdims=True) for hit in hits], axis=0)
    ranks = dot(rows.astype(jnp.bfloat16), earlier)
    pick = jnp.concatenate(
        [
            jnp.where(slot == ranks[e : e + 1], rows[e : e + 1], 0.0)
            for e in range(experts)
        ],
        axis=0,
    )
    pick_ref[...] = pick.astype(jnp.bfloat16)
    gate_values = route_scale * scores / jnp.sum(scores, axis=0, keepdims=True)
    weight = jnp.sum(gate_values * sum(hits), axis=0, keepdims=True)
    weight_ref[...] = jnp.sum(pick * weight, axis=1, keepdims=True)
    pick = pick.astype(jnp.bfloat16)
    parts = []
    for q in range(STACK):
        copies[q].wait()
        parts.append(dot(pick, tokens[q]).astype(jnp.bfloat16))
    for e in range(experts):
        outs[e][...] = jnp.concatenate([p[e * CAP : (e + 1) * CAP] for p in parts], axis=0)


def load_kernel(gate_hbm, up_hbm, down_hbm, gate, up, down, sems):
    width = gate.shape[1]
    copies = []
    for q in range(STACK):
        span = pl.ds(q * width, width)
        copies += [
            pltpu.make_async_copy(gate_hbm.at[0, span], gate.at[q], sems.at[0, q]),
            pltpu.make_async_copy(up_hbm.at[0, span], up.at[q], sems.at[1, q]),
            pltpu.make_async_copy(down_hbm.at[0, :, span], down.at[q], sems.at[2, q]),
        ]
    for copy in copies:
        copy.start()
    for copy in copies:
        copy.wait()


def expert_kernel(gate, up, down, *refs):
    count = len(refs) // 2
    blocks, outs = refs[:count], refs[count:]
    values = [block[...] for block in blocks]
    gate_part = up_part = None
    for q in range(STACK):
        rows = jnp.concatenate([pieces_of(value, q) for value in values], axis=0)
        gate_term = dot(rows, gate[q])
        up_term = dot(rows, up[q])
        gate_part = gate_term if gate_part is None else gate_part + gate_term
        up_part = up_term if up_part is None else up_part + up_term
    hidden = gate_part / (1.0 + jnp.exp(-gate_part)) * up_part
    hidden = hidden.astype(jnp.bfloat16)
    parts = [dot(hidden, down[q]).astype(jnp.bfloat16) for q in range(STACK)]
    for b in range(count):
        outs[b][...] = jnp.concatenate([p[b * CAP : (b + 1) * CAP] for p in parts], axis=0)


def final_kernel(pick_ref, weight_ref, *refs):
    blocks, out_hbm, (out, sems) = refs[:-3], refs[-3], refs[-2:]
    width = blocks[0].shape[1]
    values = [block[...] for block in blocks]
    pick = pick_ref[...]
    copies = []
    for q in range(STACK):
        rows = jnp.concatenate([pieces_of(value, q) for value in values], axis=0)
        rows = (rows.astype(jnp.float32) * weight_ref[...]).astype(jnp.bfloat16)
        placed = lax.dot_general(
            pick, rows, (((0,), (0,)), ((), ())), preferred_element_type=jnp.float32
        )
        out[q] = placed.astype(jnp.bfloat16)
        copies.append(
            pltpu.make_async_copy(
                out.at[q], out_hbm.at[:, pl.ds(q * width, width)], sems.at[q]
            )
        )
        copies[q].start()
    for copy in copies:
        copy.wait()


def in_hbm(value):
    return pltpu.with_memory_space_constraint(value, pltpu.HBM)


def after(value, done):
    done = [d[0] if isinstance(d, (list, tuple)) else d for d in done]
    return lax.optimization_barrier((value, *done))[0] if done else value


def total(*terms):
    summed = terms[0].astype(jnp.float32)
    for term in terms[1:]:
        summed = summed + term.astype(jnp.float32)
    return summed.astype(jnp.bfloat16)


def local(tokens, expert_ids, route_scores, gate_weight, up_weight, down_weight):
    token_count, model_width = tokens.shape
    hidden_width = gate_weight.shape[2]
    nodes = lax.axis_size("node")
    places = lax.axis_size("local")
    teams = places // TEAM
    flight = nodes * teams
    node = lax.axis_index("node")
    team = lax.axis_index("local") // TEAM
    width = model_width // STACK
    block = jax.ShapeDtypeStruct((STACK * CAP, width), jnp.bfloat16)

    offsets = [(n, d) for n in range(nodes) for d in range(teams)]
    flight_ids = jnp.stack(
        [((node + n) % nodes * teams + (team + d) % teams) * GSIZE for n, d in offsets]
    ).astype(jnp.int32)
    packed = pl.pallas_call(
        pack_kernel,
        out_shape=[block] * flight
        + [
            jax.ShapeDtypeStruct((flight * CAP, token_count), jnp.bfloat16),
            jax.ShapeDtypeStruct((flight * CAP, 1), jnp.float32),
        ],
        in_specs=[SMEM] + [HBM] * 3,
        out_specs=[VMEM] * (flight + 2),
        scratch_shapes=[
            pltpu.VMEM((STACK, token_count, width), jnp.bfloat16),
            pltpu.VMEM(expert_ids.shape[::-1], jnp.int32),
            pltpu.VMEM(route_scores.shape[::-1], jnp.float32),
            pltpu.SemaphoreType.DMA((STACK + 2,)),
        ],
        compiler_params=params(20),
        name="pack",
    )(flight_ids, in_hbm(expert_ids.T), in_hbm(route_scores.T), in_hbm(tokens))
    pick, weight = packed[flight:]
    packed = dict(zip(offsets, packed))

    def load(gate):
        return pl.pallas_call(
            load_kernel,
            out_shape=[
                pltpu.VMEM((STACK, width, hidden_width), jnp.bfloat16),
                pltpu.VMEM((STACK, width, hidden_width), jnp.bfloat16),
                pltpu.VMEM((STACK, hidden_width, width), jnp.bfloat16),
            ],
            in_specs=[HBM] * 3,
            out_specs=[VMEM] * 3,
            scratch_shapes=[pltpu.SemaphoreType.DMA((3, STACK))],
            compiler_params=params(20),
            cost_estimate=cost(0),
            name="load",
        )(in_hbm(gate), in_hbm(up_weight), in_hbm(down_weight))

    def experts(*operands):
        blocks, weights = operands[:-1], operands[-1]
        return pl.pallas_call(
            expert_kernel,
            out_shape=[block] * len(blocks),
            in_specs=[VMEM] * (3 + len(blocks)),
            out_specs=[VMEM] * len(blocks),
            compiler_params=params(20),
            cost_estimate=cost(len(blocks)),
            name="experts",
        )(*weights, *blocks)

    def cost(blocks):
        return pl.CostEstimate(
            flops=COST * blocks * CAP * model_width * hidden_width,
            bytes_accessed=COST * model_width * hidden_width,
            transcendentals=0,
        )

    def send(value, n, d, flip):
        pairs = [
            (
                i * places + j,
                (i + n) % nodes * places + ((j + d * TEAM) % places ^ flip),
            )
            for i in range(nodes)
            for j in range(places)
        ]
        return lax.ppermute(value, ("node", "local"), pairs)

    def along_y(value):
        return send(value, 0, 0, 1)

    def along_z(value):
        return send(value, 0, 0, 2)

    fars = [(n, d) for d in range(1, teams) for n in range(nodes)]
    steps = {"load": (load, ("gate",))}
    values = {"gate": gate_weight}
    for n in range(nodes):
        at = str(n)
        values["row_own" + at] = packed[n, 0]
        steps["own" + at] = (
            (lambda v, n=n: send(v, n, 0, 0)) if n else (lambda v: v),
            ("row_own" + at,),
        )
        steps["own_y" + at] = (along_y, ("own" + at,))
        steps["own_z" + at] = (along_z, ("own" + at,))
        steps["own_d" + at] = (along_y, ("own_z" + at,)) if n % 2 else (along_z, ("own_y" + at,))
    for i, (n, d) in enumerate(fars):
        far = "far%d" % i
        values["row_" + far] = packed[n, d]
        steps[far] = (lambda v, n=n, d=d: send(v, n, d, 0), ("row_" + far,))
        steps[far + "_y"] = (along_y, (far,))
        steps[far + "_z"] = (along_z, (far,))
        steps[far + "_d"] = (along_y, (far + "_z",))
    sides = ("", "_y", "_z", "_d")
    steps["own_experts"] = (
        experts,
        (*[v + str(n) for n in range(nodes) for v in ("own", "own_y", "own_z", "own_d")], "load"),
    )
    for i, (n, d) in enumerate(fars):
        far, back = "far%d" % i, "back%d" % i
        steps[far + "_experts"] = (experts, (*[far + v for v in sides], "load"))
        for j, v in enumerate(sides):
            steps[far + "_out" + v] = (lambda out, j=j: out[j], (far + "_experts",))
        steps[back + "_d"] = (along_y, (far + "_out_d",))
        steps[back + "_y"] = (along_y, (far + "_out_y",))
        steps[back + "_zsum"] = (total, (far + "_out_z", back + "_d"))
        steps[back + "_z"] = (along_z, (back + "_zsum",))
        steps[back + "_sum"] = (total, (far + "_out", back + "_y", back + "_z"))
        steps[back] = (lambda v, n=n, d=d: send(v, nodes - n, teams - d, 0), (back + "_sum",))
    for n in range(nodes):
        at = str(n)
        for j, v in enumerate(sides):
            steps["own_out" + v + at] = (lambda out, j=n * TEAM + j: out[j], ("own_experts",))
        first, second = ("z", "y") if n % 2 else ("y", "z")
        steps["mine_d" + at] = (along_y if n % 2 else along_z, ("own_out_d" + at,))
        steps["mine_sum" + at] = (total, ("own_out_" + first + at, "mine_d" + at))
        along = {"y": along_y, "z": along_z}
        steps["mine_" + first + at] = (along[first], ("mine_sum" + at,))
        steps["mine_" + second + at] = (along[second], ("own_out_" + second + at,))
        steps["mine" + at] = (total, ("own_out" + at, "mine_y" + at, "mine_z" + at))
        steps["home" + at] = (
            (lambda v, n=n: send(v, nodes - n, 0, 0)) if n else (lambda v: v),
            ("mine" + at,),
        )

    def value(name):
        if name not in values:
            run, takes = steps[name]
            first, *others = [value(take) for take in takes]
            done = [value(other) for other in AFTER.get(name, ()) if other in steps]
            with jax.named_scope(name):
                values[name] = run(after(first, done), *others)
        return values[name]

    returned = [
        value("home%d" % n) if d == 0 else value("back%d" % fars.index((n, d)))
        for n, d in offsets
    ]
    return pl.pallas_call(
        final_kernel,
        out_shape=jax.ShapeDtypeStruct(tokens.shape, jnp.bfloat16),
        in_specs=[VMEM] * (2 + flight),
        out_specs=pl.BlockSpec(memory_space=pltpu.HBM),
        scratch_shapes=[
            pltpu.VMEM((STACK, token_count, width), jnp.bfloat16),
            pltpu.SemaphoreType.DMA((STACK,)),
        ],
        compiler_params=params(20),
        name="combine",
    )(pick, weight, *returned)


def solution(mesh):
    in_specs = (
        P(("rep", "node", "local"), None),
        P(("rep", "node", "local"), None),
        P(("rep", "node", "local"), None),
        P(("node", "local"), None, None),
        P(("node", "local"), None, None),
        P(("node", "local"), None, None),
    )
    out_specs = P(("rep", "node", "local"), None)
    return jax.shard_map(local, mesh=mesh, in_specs=in_specs, out_specs=out_specs, check_vma=False)
```

```python
import jax
import jax.numpy as jnp
from jax import lax
from jax.experimental import pallas as pl
from jax.experimental.pallas import tpu as pltpu
from jax.sharding import PartitionSpec as P

TEAM = 4
CAP = 18
GSIZE = 32
STACK = 4
COST = 15

HOPS = {"own": "yy", "far": "zy", "mine": "zy", "back": "yy"}

AFTER = {
    "load": ("own1",),
    "own_z0": ("own1",),
    "own_d0": ("far0_y",),
    "own_d1": ("own_y1",),
    "far0_d": ("own_z0",),
    "far0_y": ("load", "own_y0", "own_y1"),
    "far0_z": ("load", "own_z0"),
    "far1": ("far0", "load"),
    "far1_d": ("own_d0",),
    "far1_experts": ("own_experts",),
    "far1_y": ("own_d1",),
    "far1_z": ("far0_z",),
    "own_experts": ("far0_experts",),
    "back0_y": ("back0_d",),
    "back1_y": ("back0_y",),
    "back1_z": ("back0_z",),
    "mine_d1": ("far1_d",),
    "mine_y0": ("back1_y",),
    "mine_y1": ("back1_y",),
    "mine_z0": ("back0_z",),
    "mine_z1": ("back0_z",),
    "home1": ("back1_z",),
}

route_scale = 2.5
VMEM = pl.BlockSpec(memory_space=pltpu.VMEM)
SMEM = pl.BlockSpec(memory_space=pltpu.SMEM)
HBM = pl.BlockSpec(memory_space=pltpu.HBM)


def dot(a, b):
    return jnp.dot(a, b, preferred_element_type=jnp.float32)


def params(mib):
    return pltpu.CompilerParams(vmem_limit_bytes=mib << 20)


def pieces_of(value, q):
    return value[q * CAP : (q + 1) * CAP]


def pack_kernel(flight_ref, ids_hbm, scores_hbm, tokens_hbm, *refs):
    tokens, ids_ref, scores_ref, sems = refs[-4:]
    outs, pick_ref, weight_ref = refs[:-6], refs[-6], refs[-5]
    experts = len(outs)
    width = outs[0].shape[1]
    copies = [
        pltpu.make_async_copy(
            tokens_hbm.at[:, pl.ds(q * width, width)], tokens.at[q], sems.at[q]
        )
        for q in range(STACK)
    ]
    small = [
        pltpu.make_async_copy(ids_hbm, ids_ref, sems.at[STACK]),
        pltpu.make_async_copy(scores_hbm, scores_ref, sems.at[STACK + 1]),
    ]
    for copy in small + copies:
        copy.start()
    for copy in small:
        copy.wait()
    ids = ids_ref[...]
    scores = scores_ref[...]
    count = ids.shape[1]
    earlier = lax.broadcasted_iota(jnp.int32, (count, count), 0) < lax.broadcasted_iota(
        jnp.int32, (count, count), 1
    )
    earlier = jnp.where(earlier, 1.0, 0.0).astype(jnp.bfloat16)
    slot = lax.broadcasted_iota(jnp.int32, (CAP, count), 0).astype(jnp.float32)
    hits = [jnp.where(ids == flight_ref[e], 1.0, 0.0) for e in range(experts)]
    rows = jnp.concatenate([jnp.sum(hit, axis=0, keepdims=True) for hit in hits], axis=0)
    ranks = dot(rows.astype(jnp.bfloat16), earlier)
    pick = jnp.concatenate(
        [
            jnp.where(slot == ranks[e : e + 1], rows[e : e + 1], 0.0)
            for e in range(experts)
        ],
        axis=0,
    )
    pick_ref[...] = pick.astype(jnp.bfloat16)
    gate_values = route_scale * scores / jnp.sum(scores, axis=0, keepdims=True)
    weight = jnp.sum(gate_values * sum(hits), axis=0, keepdims=True)
    weight_ref[...] = jnp.sum(pick * weight, axis=1, keepdims=True)
    pick = pick.astype(jnp.bfloat16)
    parts = []
    for q in range(STACK):
        copies[q].wait()
        parts.append(dot(pick, tokens[q]).astype(jnp.bfloat16))
    for e in range(experts):
        outs[e][...] = jnp.concatenate([p[e * CAP : (e + 1) * CAP] for p in parts], axis=0)


def load_kernel(gate_hbm, up_hbm, down_hbm, gate, up, down, sems):
    width = gate.shape[1]
    copies = []
    for q in range(STACK):
        span = pl.ds(q * width, width)
        copies += [
            pltpu.make_async_copy(gate_hbm.at[0, span], gate.at[q], sems.at[0, q]),
            pltpu.make_async_copy(up_hbm.at[0, span], up.at[q], sems.at[1, q]),
            pltpu.make_async_copy(down_hbm.at[0, :, span], down.at[q], sems.at[2, q]),
        ]
    for copy in copies:
        copy.start()
    for copy in copies:
        copy.wait()


def expert_kernel(gate, up, down, *refs):
    count = len(refs) // 2
    blocks, outs = refs[:count], refs[count:]
    values = [block[...] for block in blocks]
    gate_part = up_part = None
    for q in range(STACK):
        rows = jnp.concatenate([pieces_of(value, q) for value in values], axis=0)
        gate_term = dot(rows, gate[q])
        up_term = dot(rows, up[q])
        gate_part = gate_term if gate_part is None else gate_part + gate_term
        up_part = up_term if up_part is None else up_part + up_term
    hidden = gate_part / (1.0 + jnp.exp(-gate_part)) * up_part
    hidden = hidden.astype(jnp.bfloat16)
    parts = [dot(hidden, down[q]).astype(jnp.bfloat16) for q in range(STACK)]
    for b in range(count):
        outs[b][...] = jnp.concatenate([p[b * CAP : (b + 1) * CAP] for p in parts], axis=0)


def final_kernel(pick_ref, weight_ref, *refs):
    blocks, out_hbm, (out, sems) = refs[:-3], refs[-3], refs[-2:]
    width = blocks[0].shape[1]
    values = [block[...] for block in blocks]
    pick = pick_ref[...]
    copies = []
    for q in range(STACK):
        rows = jnp.concatenate([pieces_of(value, q) for value in values], axis=0)
        rows = (rows.astype(jnp.float32) * weight_ref[...]).astype(jnp.bfloat16)
        placed = lax.dot_general(
            pick, rows, (((0,), (0,)), ((), ())), preferred_element_type=jnp.float32
        )
        out[q] = placed.astype(jnp.bfloat16)
        copies.append(
            pltpu.make_async_copy(
                out.at[q], out_hbm.at[:, pl.ds(q * width, width)], sems.at[q]
            )
        )
        copies[q].start()
    for copy in copies:
        copy.wait()


def in_hbm(value):
    return pltpu.with_memory_space_constraint(value, pltpu.HBM)


def after(value, done):
    done = [d[0] if isinstance(d, (list, tuple)) else d for d in done]
    return lax.optimization_barrier((value, *done))[0] if done else value


def total(*terms):
    summed = terms[0].astype(jnp.float32)
    for term in terms[1:]:
        summed = summed + term.astype(jnp.float32)
    return summed.astype(jnp.bfloat16)


def local(tokens, expert_ids, route_scores, gate_weight, up_weight, down_weight):
    token_count, model_width = tokens.shape
    hidden_width = gate_weight.shape[2]
    nodes = lax.axis_size("node")
    places = lax.axis_size("local")
    teams = places // TEAM
    flight = nodes * teams
    node = lax.axis_index("node")
    team = lax.axis_index("local") // TEAM
    width = model_width // STACK
    block = jax.ShapeDtypeStruct((STACK * CAP, width), jnp.bfloat16)

    offsets = [(n, d) for n in range(nodes) for d in range(teams)]
    flight_ids = jnp.stack(
        [((node + n) % nodes * teams + (team + d) % teams) * GSIZE for n, d in offsets]
    ).astype(jnp.int32)
    packed = pl.pallas_call(
        pack_kernel,
        out_shape=[block] * flight
        + [
            jax.ShapeDtypeStruct((flight * CAP, token_count), jnp.bfloat16),
            jax.ShapeDtypeStruct((flight * CAP, 1), jnp.float32),
        ],
        in_specs=[SMEM] + [HBM] * 3,
        out_specs=[VMEM] * (flight + 2),
        scratch_shapes=[
            pltpu.VMEM((STACK, token_count, width), jnp.bfloat16),
            pltpu.VMEM(expert_ids.shape[::-1], jnp.int32),
            pltpu.VMEM(route_scores.shape[::-1], jnp.float32),
            pltpu.SemaphoreType.DMA((STACK + 2,)),
        ],
        compiler_params=params(20),
        name="pack",
    )(flight_ids, in_hbm(expert_ids.T), in_hbm(route_scores.T), in_hbm(tokens))
    pick, weight = packed[flight:]
    packed = dict(zip(offsets, packed))

    def load(gate):
        return pl.pallas_call(
            load_kernel,
            out_shape=[
                pltpu.VMEM((STACK, width, hidden_width), jnp.bfloat16),
                pltpu.VMEM((STACK, width, hidden_width), jnp.bfloat16),
                pltpu.VMEM((STACK, hidden_width, width), jnp.bfloat16),
            ],
            in_specs=[HBM] * 3,
            out_specs=[VMEM] * 3,
            scratch_shapes=[pltpu.SemaphoreType.DMA((3, STACK))],
            compiler_params=params(20),
            cost_estimate=cost(0),
            name="load",
        )(in_hbm(gate), in_hbm(up_weight), in_hbm(down_weight))

    def experts(*operands):
        blocks, weights = operands[:-1], operands[-1]
        return pl.pallas_call(
            expert_kernel,
            out_shape=[block] * len(blocks),
            in_specs=[VMEM] * (3 + len(blocks)),
            out_specs=[VMEM] * len(blocks),
            compiler_params=params(20),
            cost_estimate=cost(len(blocks)),
            name="experts",
        )(*weights, *blocks)

    def cost(blocks):
        return pl.CostEstimate(
            flops=COST * blocks * CAP * model_width * hidden_width,
            bytes_accessed=COST * model_width * hidden_width,
            transcendentals=0,
        )

    def send(value, n, d, flip):
        pairs = [
            (
                i * places + j,
                (i + n) % nodes * places + ((j + d * TEAM) % places ^ flip),
            )
            for i in range(nodes)
            for j in range(places)
        ]
        return lax.ppermute(value, ("node", "local"), pairs)

    def along_y(value):
        return send(value, 0, 0, 1)

    def along_z(value):
        return send(value, 0, 0, 2)

    along = {"y": along_y, "z": along_z}

    def hops(kind, i):
        hop = HOPS[kind][i % 2]
        return hop, "z" if hop == "y" else "y"

    fars = [(n, d) for d in range(1, teams) for n in range(nodes)]
    steps = {"load": (load, ("gate",))}
    values = {"gate": gate_weight}
    for n in range(nodes):
        at = str(n)
        values["row_own" + at] = packed[n, 0]
        steps["own" + at] = (
            (lambda v, n=n: send(v, n, 0, 0)) if n else (lambda v: v),
            ("row_own" + at,),
        )
        steps["own_y" + at] = (along_y, ("own" + at,))
        steps["own_z" + at] = (along_z, ("own" + at,))
        hop, turn = hops("own", n)
        steps["own_d" + at] = (along[hop], ("own_" + turn + at,))
    for i, (n, d) in enumerate(fars):
        far = "far%d" % i
        values["row_" + far] = packed[n, d]
        steps[far] = (lambda v, n=n, d=d: send(v, n, d, 0), ("row_" + far,))
        steps[far + "_y"] = (along_y, (far,))
        steps[far + "_z"] = (along_z, (far,))
        hop, turn = hops("far", i)
        steps[far + "_d"] = (along[hop], (far + "_" + turn,))
    sides = ("", "_y", "_z", "_d")
    steps["own_experts"] = (
        experts,
        (*[v + str(n) for n in range(nodes) for v in ("own", "own_y", "own_z", "own_d")], "load"),
    )
    for i, (n, d) in enumerate(fars):
        far, back = "far%d" % i, "back%d" % i
        steps[far + "_experts"] = (experts, (*[far + v for v in sides], "load"))
        for j, v in enumerate(sides):
            steps[far + "_out" + v] = (lambda out, j=j: out[j], (far + "_experts",))
        hop, turn = hops("back", i)
        steps[back + "_d"] = (along[hop], (far + "_out_d",))
        steps[back + "_" + hop] = (along[hop], (far + "_out_" + hop,))
        steps[back + "_turn"] = (total, (far + "_out_" + turn, back + "_d"))
        steps[back + "_" + turn] = (along[turn], (back + "_turn",))
        steps[back + "_sum"] = (total, (far + "_out", back + "_y", back + "_z"))
        steps[back] = (lambda v, n=n, d=d: send(v, nodes - n, teams - d, 0), (back + "_sum",))
    for n in range(nodes):
        at = str(n)
        for j, v in enumerate(sides):
            steps["own_out" + v + at] = (lambda out, j=n * TEAM + j: out[j], ("own_experts",))
        hop, turn = hops("mine", n)
        steps["mine_d" + at] = (along[hop], ("own_out_d" + at,))
        steps["mine_" + hop + at] = (along[hop], ("own_out_" + hop + at,))
        steps["mine_turn" + at] = (total, ("own_out_" + turn + at, "mine_d" + at))
        steps["mine_" + turn + at] = (along[turn], ("mine_turn" + at,))
        steps["mine" + at] = (total, ("own_out" + at, "mine_y" + at, "mine_z" + at))
        steps["home" + at] = (
            (lambda v, n=n: send(v, nodes - n, 0, 0)) if n else (lambda v: v),
            ("mine" + at,),
        )

    def value(name):
        if name not in values:
            run, takes = steps[name]
            first, *others = [value(take) for take in takes]
            done = [value(other) for other in AFTER.get(name, ()) if other in steps]
            with jax.named_scope(name):
                values[name] = run(after(first, done), *others)
        return values[name]

    returned = [
        value("home%d" % n) if d == 0 else value("back%d" % fars.index((n, d)))
        for n, d in offsets
    ]
    return pl.pallas_call(
        final_kernel,
        out_shape=jax.ShapeDtypeStruct(tokens.shape, jnp.bfloat16),
        in_specs=[VMEM] * (2 + flight),
        out_specs=pl.BlockSpec(memory_space=pltpu.HBM),
        scratch_shapes=[
            pltpu.VMEM((STACK, token_count, width), jnp.bfloat16),
            pltpu.SemaphoreType.DMA((STACK,)),
        ],
        compiler_params=params(20),
        name="combine",
    )(pick, weight, *returned)


def solution(mesh):
    in_specs = (
        P(("rep", "node", "local"), None),
        P(("rep", "node", "local"), None),
        P(("rep", "node", "local"), None),
        P(("node", "local"), None, None),
        P(("node", "local"), None, None),
        P(("node", "local"), None, None),
    )
    out_specs = P(("rep", "node", "local"), None)
    return jax.shard_map(local, mesh=mesh, in_specs=in_specs, out_specs=out_specs, check_vma=False)
```

```python
import jax
import jax.numpy as jnp
from jax import lax
from jax.experimental import pallas as pl
from jax.experimental.pallas import tpu as pltpu
from jax.sharding import PartitionSpec as P

TEAM = 4
CAP = 18
GSIZE = 32
STACK = 4
COST = 15

HOPS = {"own": "yy", "far": "zy", "mine": "zy", "back": "zy"}

AFTER = {
    "load": ("own1",),
    "own_z0": ("own1",),
    "own_d0": ("far0_y",),
    "own_d1": ("own_y1",),
    "far0_d": ("own_z0",),
    "far0_y": ("load", "own_y0", "own_y1"),
    "far0_z": ("load", "own_z0"),
    "far1": ("far0", "load"),
    "far1_d": ("own_d0",),
    "far1_experts": ("own_experts",),
    "far1_y": ("own_d1",),
    "far1_z": ("far0_z",),
    "own_experts": ("far0_experts",),
    "back0_y": ("back0_d",),
    "back0_z": ("back0_d",),
    "back1_y": ("back0_y",),
    "back1_z": ("back0_z",),
    "mine_d1": ("far1_d",),
    "mine_y0": ("back1_y",),
    "mine_y1": ("back1_y",),
    "mine_z0": ("back1_z",),
    "mine_z1": ("back0_z",),
    "home1": ("back1_z",),
}

route_scale = 2.5
VMEM = pl.BlockSpec(memory_space=pltpu.VMEM)
SMEM = pl.BlockSpec(memory_space=pltpu.SMEM)
HBM = pl.BlockSpec(memory_space=pltpu.HBM)


def dot(a, b):
    return jnp.dot(a, b, preferred_element_type=jnp.float32)


def params(mib):
    return pltpu.CompilerParams(vmem_limit_bytes=mib << 20)


def pieces_of(value, q):
    return value[q * CAP : (q + 1) * CAP]


def pack_kernel(flight_ref, ids_hbm, scores_hbm, tokens_hbm, *refs):
    tokens, ids_ref, scores_ref, sems = refs[-4:]
    outs, pick_ref, weight_ref = refs[:-6], refs[-6], refs[-5]
    experts = len(outs)
    width = outs[0].shape[1]
    copies = [
        pltpu.make_async_copy(
            tokens_hbm.at[:, pl.ds(q * width, width)], tokens.at[q], sems.at[q]
        )
        for q in range(STACK)
    ]
    small = [
        pltpu.make_async_copy(ids_hbm, ids_ref, sems.at[STACK]),
        pltpu.make_async_copy(scores_hbm, scores_ref, sems.at[STACK + 1]),
    ]
    for copy in small + copies:
        copy.start()
    for copy in small:
        copy.wait()
    ids = ids_ref[...]
    scores = scores_ref[...]
    count = ids.shape[1]
    earlier = lax.broadcasted_iota(jnp.int32, (count, count), 0) < lax.broadcasted_iota(
        jnp.int32, (count, count), 1
    )
    earlier = jnp.where(earlier, 1.0, 0.0).astype(jnp.bfloat16)
    slot = lax.broadcasted_iota(jnp.int32, (CAP, count), 0).astype(jnp.float32)
    hits = [jnp.where(ids == flight_ref[e], 1.0, 0.0) for e in range(experts)]
    rows = jnp.concatenate([jnp.sum(hit, axis=0, keepdims=True) for hit in hits], axis=0)
    ranks = dot(rows.astype(jnp.bfloat16), earlier)
    pick = jnp.concatenate(
        [
            jnp.where(slot == ranks[e : e + 1], rows[e : e + 1], 0.0)
            for e in range(experts)
        ],
        axis=0,
    )
    pick_ref[...] = pick.astype(jnp.bfloat16)
    gate_values = route_scale * scores / jnp.sum(scores, axis=0, keepdims=True)
    weight = jnp.sum(gate_values * sum(hits), axis=0, keepdims=True)
    weight_ref[...] = jnp.sum(pick * weight, axis=1, keepdims=True)
    pick = pick.astype(jnp.bfloat16)
    parts = []
    for q in range(STACK):
        copies[q].wait()
        parts.append(dot(pick, tokens[q]).astype(jnp.bfloat16))
    for e in range(experts):
        outs[e][...] = jnp.concatenate([p[e * CAP : (e + 1) * CAP] for p in parts], axis=0)


def load_kernel(gate_hbm, up_hbm, down_hbm, gate, up, down, sems):
    width = gate.shape[1]
    copies = []
    for q in range(STACK):
        span = pl.ds(q * width, width)
        copies += [
            pltpu.make_async_copy(gate_hbm.at[0, span], gate.at[q], sems.at[0, q]),
            pltpu.make_async_copy(up_hbm.at[0, span], up.at[q], sems.at[1, q]),
            pltpu.make_async_copy(down_hbm.at[0, :, span], down.at[q], sems.at[2, q]),
        ]
    for copy in copies:
        copy.start()
    for copy in copies:
        copy.wait()


def expert_kernel(gate, up, down, *refs):
    count = len(refs) // 2
    blocks, outs = refs[:count], refs[count:]
    values = [block[...] for block in blocks]
    gate_part = up_part = None
    for q in range(STACK):
        rows = jnp.concatenate([pieces_of(value, q) for value in values], axis=0)
        gate_term = dot(rows, gate[q])
        up_term = dot(rows, up[q])
        gate_part = gate_term if gate_part is None else gate_part + gate_term
        up_part = up_term if up_part is None else up_part + up_term
    hidden = gate_part / (1.0 + jnp.exp(-gate_part)) * up_part
    hidden = hidden.astype(jnp.bfloat16)
    parts = [dot(hidden, down[q]).astype(jnp.bfloat16) for q in range(STACK)]
    for b in range(count):
        outs[b][...] = jnp.concatenate([p[b * CAP : (b + 1) * CAP] for p in parts], axis=0)


def final_kernel(pick_ref, weight_ref, *refs):
    blocks, out_hbm, (out, sems) = refs[:-3], refs[-3], refs[-2:]
    width = blocks[0].shape[1]
    values = [block[...] for block in blocks]
    pick = pick_ref[...]
    copies = []
    for q in range(STACK):
        rows = jnp.concatenate([pieces_of(value, q) for value in values], axis=0)
        rows = (rows.astype(jnp.float32) * weight_ref[...]).astype(jnp.bfloat16)
        placed = lax.dot_general(
            pick, rows, (((0,), (0,)), ((), ())), preferred_element_type=jnp.float32
        )
        out[q] = placed.astype(jnp.bfloat16)
        copies.append(
            pltpu.make_async_copy(
                out.at[q], out_hbm.at[:, pl.ds(q * width, width)], sems.at[q]
            )
        )
        copies[q].start()
    for copy in copies:
        copy.wait()


def in_hbm(value):
    return pltpu.with_memory_space_constraint(value, pltpu.HBM)


def after(value, done):
    done = [d[0] if isinstance(d, (list, tuple)) else d for d in done]
    return lax.optimization_barrier((value, *done))[0] if done else value


def total(*terms):
    summed = terms[0].astype(jnp.float32)
    for term in terms[1:]:
        summed = summed + term.astype(jnp.float32)
    return summed.astype(jnp.bfloat16)


def local(tokens, expert_ids, route_scores, gate_weight, up_weight, down_weight):
    token_count, model_width = tokens.shape
    hidden_width = gate_weight.shape[2]
    nodes = lax.axis_size("node")
    places = lax.axis_size("local")
    teams = places // TEAM
    flight = nodes * teams
    node = lax.axis_index("node")
    team = lax.axis_index("local") // TEAM
    width = model_width // STACK
    block = jax.ShapeDtypeStruct((STACK * CAP, width), jnp.bfloat16)

    offsets = [(n, d) for n in range(nodes) for d in range(teams)]
    flight_ids = jnp.stack(
        [((node + n) % nodes * teams + (team + d) % teams) * GSIZE for n, d in offsets]
    ).astype(jnp.int32)
    packed = pl.pallas_call(
        pack_kernel,
        out_shape=[block] * flight
        + [
            jax.ShapeDtypeStruct((flight * CAP, token_count), jnp.bfloat16),
            jax.ShapeDtypeStruct((flight * CAP, 1), jnp.float32),
        ],
        in_specs=[SMEM] + [HBM] * 3,
        out_specs=[VMEM] * (flight + 2),
        scratch_shapes=[
            pltpu.VMEM((STACK, token_count, width), jnp.bfloat16),
            pltpu.VMEM(expert_ids.shape[::-1], jnp.int32),
            pltpu.VMEM(route_scores.shape[::-1], jnp.float32),
            pltpu.SemaphoreType.DMA((STACK + 2,)),
        ],
        compiler_params=params(20),
        name="pack",
    )(flight_ids, in_hbm(expert_ids.T), in_hbm(route_scores.T), in_hbm(tokens))
    pick, weight = packed[flight:]
    packed = dict(zip(offsets, packed))

    def load(gate):
        return pl.pallas_call(
            load_kernel,
            out_shape=[
                pltpu.VMEM((STACK, width, hidden_width), jnp.bfloat16),
                pltpu.VMEM((STACK, width, hidden_width), jnp.bfloat16),
                pltpu.VMEM((STACK, hidden_width, width), jnp.bfloat16),
            ],
            in_specs=[HBM] * 3,
            out_specs=[VMEM] * 3,
            scratch_shapes=[pltpu.SemaphoreType.DMA((3, STACK))],
            compiler_params=params(20),
            cost_estimate=cost(0),
            name="load",
        )(in_hbm(gate), in_hbm(up_weight), in_hbm(down_weight))

    def experts(*operands):
        blocks, weights = operands[:-1], operands[-1]
        return pl.pallas_call(
            expert_kernel,
            out_shape=[block] * len(blocks),
            in_specs=[VMEM] * (3 + len(blocks)),
            out_specs=[VMEM] * len(blocks),
            compiler_params=params(20),
            cost_estimate=cost(len(blocks)),
            name="experts",
        )(*weights, *blocks)

    def cost(blocks):
        return pl.CostEstimate(
            flops=COST * blocks * CAP * model_width * hidden_width,
            bytes_accessed=COST * model_width * hidden_width,
            transcendentals=0,
        )

    def send(value, n, d, flip):
        pairs = [
            (
                i * places + j,
                (i + n) % nodes * places + ((j + d * TEAM) % places ^ flip),
            )
            for i in range(nodes)
            for j in range(places)
        ]
        return lax.ppermute(value, ("node", "local"), pairs)

    def along_y(value):
        return send(value, 0, 0, 1)

    def along_z(value):
        return send(value, 0, 0, 2)

    along = {"y": along_y, "z": along_z}

    def hops(kind, i):
        hop = HOPS[kind][i % 2]
        return hop, "z" if hop == "y" else "y"

    fars = [(n, d) for d in range(1, teams) for n in range(nodes)]
    steps = {"load": (load, ("gate",))}
    values = {"gate": gate_weight}
    for n in range(nodes):
        at = str(n)
        values["row_own" + at] = packed[n, 0]
        steps["own" + at] = (
            (lambda v, n=n: send(v, n, 0, 0)) if n else (lambda v: v),
            ("row_own" + at,),
        )
        steps["own_y" + at] = (along_y, ("own" + at,))
        steps["own_z" + at] = (along_z, ("own" + at,))
        hop, turn = hops("own", n)
        steps["own_d" + at] = (along[hop], ("own_" + turn + at,))
    for i, (n, d) in enumerate(fars):
        far = "far%d" % i
        values["row_" + far] = packed[n, d]
        steps[far] = (lambda v, n=n, d=d: send(v, n, d, 0), ("row_" + far,))
        steps[far + "_y"] = (along_y, (far,))
        steps[far + "_z"] = (along_z, (far,))
        hop, turn = hops("far", i)
        steps[far + "_d"] = (along[hop], (far + "_" + turn,))
    sides = ("", "_y", "_z", "_d")
    steps["own_experts"] = (
        experts,
        (*[v + str(n) for n in range(nodes) for v in ("own", "own_y", "own_z", "own_d")], "load"),
    )
    for i, (n, d) in enumerate(fars):
        far, back = "far%d" % i, "back%d" % i
        steps[far + "_experts"] = (experts, (*[far + v for v in sides], "load"))
        for j, v in enumerate(sides):
            steps[far + "_out" + v] = (lambda out, j=j: out[j], (far + "_experts",))
        hop, turn = hops("back", i)
        steps[back + "_d"] = (along[hop], (far + "_out_d",))
        steps[back + "_" + hop] = (along[hop], (far + "_out_" + hop,))
        steps[back + "_turn"] = (total, (far + "_out_" + turn, back + "_d"))
        steps[back + "_" + turn] = (along[turn], (back + "_turn",))
        steps[back + "_sum"] = (total, (far + "_out", back + "_y", back + "_z"))
        steps[back] = (lambda v, n=n, d=d: send(v, nodes - n, teams - d, 0), (back + "_sum",))
    for n in range(nodes):
        at = str(n)
        for j, v in enumerate(sides):
            steps["own_out" + v + at] = (lambda out, j=n * TEAM + j: out[j], ("own_experts",))
        hop, turn = hops("mine", n)
        steps["mine_d" + at] = (along[hop], ("own_out_d" + at,))
        steps["mine_" + hop + at] = (along[hop], ("own_out_" + hop + at,))
        steps["mine_turn" + at] = (total, ("own_out_" + turn + at, "mine_d" + at))
        steps["mine_" + turn + at] = (along[turn], ("mine_turn" + at,))
        steps["mine" + at] = (total, ("own_out" + at, "mine_y" + at, "mine_z" + at))
        steps["home" + at] = (
            (lambda v, n=n: send(v, nodes - n, 0, 0)) if n else (lambda v: v),
            ("mine" + at,),
        )

    def value(name):
        if name not in values:
            run, takes = steps[name]
            first, *others = [value(take) for take in takes]
            done = [value(other) for other in AFTER.get(name, ()) if other in steps]
            with jax.named_scope(name):
                values[name] = run(after(first, done), *others)
        return values[name]

    returned = [
        value("home%d" % n) if d == 0 else value("back%d" % fars.index((n, d)))
        for n, d in offsets
    ]
    return pl.pallas_call(
        final_kernel,
        out_shape=jax.ShapeDtypeStruct(tokens.shape, jnp.bfloat16),
        in_specs=[VMEM] * (2 + flight),
        out_specs=pl.BlockSpec(memory_space=pltpu.HBM),
        scratch_shapes=[
            pltpu.VMEM((STACK, token_count, width), jnp.bfloat16),
            pltpu.SemaphoreType.DMA((STACK,)),
        ],
        compiler_params=params(20),
        name="combine",
    )(pick, weight, *returned)


def solution(mesh):
    in_specs = (
        P(("rep", "node", "local"), None),
        P(("rep", "node", "local"), None),
        P(("rep", "node", "local"), None),
        P(("node", "local"), None, None),
        P(("node", "local"), None, None),
        P(("node", "local"), None, None),
    )
    out_specs = P(("rep", "node", "local"), None)
    return jax.shard_map(local, mesh=mesh, in_specs=in_specs, out_specs=out_specs, check_vma=False)
```
